128 devices in a mesh: var: 8 (over x_hi, z), seq: 16 (over x_lo, y, core).
Axes of the slice: x: 4 (x_hi: 2, x_lo: 2; x = x_hi * 2 + x_lo), y: 4, z: 4, core: 2. Of those that a mesh axis runs over, the one named last changes fastest.
Arguments:
- fields: bfloat16 [48, 4096, 1024], P('var', 'seq'), may hold values from -10 to 10
- var_bias: bfloat16 [48, 1024], P('var'), may hold values from -3 to 3
- agg_score: bfloat16 [1024, 16], replicated
- agg_value: bfloat16 [1024, 1024], P('seq'), may hold values from -0.1875 to 0.1875
- agg_out: bfloat16 [1024, 4096], P(None, 'var'), may hold values from -0.1875 to 0.1875
- norm_gain: float32 [4096], replicated, may hold values from 0.5 to 1.5
- w_query: bfloat16 [4096, 4096], P(None, 'var')
- w_key: bfloat16 [4096, 4096], P(None, 'var')
- w_value: bfloat16 [4096, 4096], P(None, 'var'), may hold values from -0.09375 to 0.09375
- w_out: bfloat16 [4096, 4096], P('var'), may hold values from -0.09375 to 0.09375
- w_back: bfloat16 [4096, 1024], P('var'), may hold values from -0.09375 to 0.09375
- var_gate: bfloat16 [48, 1024], P('var'), may hold values from 0.5 to 1.5
Outputs:
- mixed: bfloat16 [4096, 4096], P('seq', 'var')
- out_fields: bfloat16 [48, 4096, 1024], P('var', 'seq')
The draws below stay inside these ranges and needn't reach their ends.
All inputs are finite; a program needn't handle non-finite values.
Results may differ from the reference program's by a relative error of at most 0.029.
Values may be sent and summed in bfloat16 or wider, within the bound.
A program may use at most 128 MiB of HBM per device.

```python
import math
import jax
import jax.numpy as jnp
from jax import lax

D = 4096
H = 32
E = 1024
HA = 16
VARS = 48
TOKENS = 4096


def sign_pattern(key):
    flips = jax.random.bernoulli(jax.random.fold_in(key, 101), 0.5, (E, HA))
    return jnp.where(flips, 1.0, -1.0).astype(jnp.float32)


def draw_agg_score(key, part):
    signs = sign_pattern(key)
    key = jax.random.fold_in(key, 3)
    size = jnp.abs(jax.random.truncated_normal(key, -4.0, 4.0, (E, HA), jnp.float32))
    return (signs * size * E ** (-0.5)).astype(jnp.bfloat16)


def draw_fields(key, part):
    key = jax.random.fold_in(key, 5)
    keys = jax.random.split(key, 1)
    base = jax.random.truncated_normal(keys[0], -6.0, 6.0, (VARS, TOKENS, E), jnp.float32)
    return base.astype(jnp.bfloat16)


def draw_w_query(key, part):
    key = jax.random.fold_in(key, 7)
    base = jax.random.truncated_normal(key, -4.0, 4.0, (D, D), jnp.float32) * D ** (-0.5)
    return base.astype(jnp.bfloat16)


def draw_w_key(key, part):
    key = jax.random.fold_in(key, 11)
    base = jax.random.truncated_normal(key, -4.0, 4.0, (D, D), jnp.float32) * D ** (-0.5)
    return base.astype(jnp.bfloat16)


def shard_levels(key, shape, shards, low, high):
    def one(axis_at, shards_of):
        heights = jax.random.uniform(jax.random.fold_in(jax.random.fold_in(key, 6), axis_at), (shards_of,), jnp.float32, low / len(shards), high / len(shards))
        return jnp.repeat(jnp.exp(heights), shape[axis_at] // shards_of).reshape((-1,) + (1,) * (len(shape) - axis_at - 1))

    gain = one(*shards[0])
    for cut in shards[1:]:
        gain = gain * one(*cut)
    return gain


def centred(stream_key, shape, scale, limit, cuts=(), held_as=jnp.bfloat16):
    entries = scale * jax.random.normal(stream_key, shape, jnp.float32)
    if cuts:
        entries = entries * shard_levels(stream_key, shape, cuts, -0.22, 0.18)
    return jnp.clip(entries, -limit, limit).astype(held_as)


def setup_inputs(seed: int = 0) -> dict:
    key_list = jax.random.split(jax.random.key(seed), 13)
    return {
        "fields": draw_fields(jax.random.fold_in(key_list[12], 71), 0),
        "var_bias": centred(key_list[1], (VARS, E), 0.5, 3.0, ((0, 8),)),
        "agg_score": draw_agg_score(jax.random.fold_in(key_list[12], 71), 0),
        "agg_value": centred(key_list[3], (E, E), E ** -0.5, 0.1875, ((0, 16),)),
        "agg_out": centred(key_list[4], (E, D), E ** -0.5, 0.1875, ((1, 8),)),
        "norm_gain": jnp.clip(1.0 + 0.1 * jax.random.normal(key_list[5], (D,), jnp.float32), 0.5, 1.5),
        "w_query": draw_w_query(jax.random.fold_in(key_list[12], 71), 0),
        "w_key": draw_w_key(jax.random.fold_in(key_list[12], 71), 0),
        "w_value": centred(key_list[8], (D, D), D ** -0.5, 0.09375, ((1, 8),)),
        "w_out": centred(key_list[9], (D, D), D ** -0.5, 0.09375, ((0, 8),)),
        "w_back": centred(key_list[10], (D, E), D ** -0.5, 0.09375, ((0, 8),)),
        "var_gate": jnp.clip(0.5 + 1.0 * jax.random.uniform(key_list[11], (VARS, E), jnp.float32) ** shard_levels(key_list[11], (VARS, E), ((0, 8),), -0.2, 0.2), 0.5, 1.5).astype(jnp.bfloat16),
    }


def reference(fields, var_bias, agg_score, agg_value, agg_out, norm_gain, w_query, w_key, w_value, w_out, w_back, var_gate):
    head_dim = D // H
    agg_dim = E // HA
    block = math.gcd(TOKENS, 512)
    blocks = TOKENS // block

    def aggregate(piece):
        embedded = (piece.astype(jnp.float32) + var_bias.astype(jnp.float32)[:, None, :]).astype(jnp.bfloat16)
        score = jnp.einsum('vte,eh->vth', embedded.astype(jnp.float32), agg_score.astype(jnp.float32))
        peak = lax.optimization_barrier(jnp.max(score, axis=0))
        prob = jnp.exp(score - peak[None])
        total = lax.optimization_barrier(jnp.sum(prob, axis=0))
        values = jnp.dot(embedded.reshape(-1, E), agg_value, preferred_element_type=jnp.float32).astype(jnp.bfloat16)
        values = values.reshape(VARS, block, HA, agg_dim)
        summed = jnp.einsum('vth,vthd->thd', prob, values.astype(jnp.float32))
        return (summed / total[:, :, None]).reshape(block, E).astype(jnp.bfloat16)
    stacked = fields.reshape(VARS, blocks, block, E).transpose(1, 0, 2, 3)
    agg = lax.map(aggregate, stacked).reshape(TOKENS, E)
    hidden = jnp.dot(agg, agg_out, preferred_element_type=jnp.float32).astype(jnp.bfloat16)
    wide = hidden.astype(jnp.float32)
    mean = lax.optimization_barrier(jnp.mean(wide, axis=1, keepdims=True))
    spread = lax.optimization_barrier(jnp.mean((wide - mean) ** 2, axis=1, keepdims=True))
    normed = ((wide - mean) * lax.rsqrt(spread + 1e-05) * norm_gain[None, :]).astype(jnp.bfloat16)
    query = jnp.dot(normed, w_query, preferred_element_type=jnp.float32).astype(jnp.bfloat16)
    keys = jnp.dot(normed, w_key, preferred_element_type=jnp.float32).astype(jnp.bfloat16)
    vals = jnp.dot(normed, w_value, preferred_element_type=jnp.float32).astype(jnp.bfloat16)

    def split_heads(matrix):
        return matrix.reshape(TOKENS, H, head_dim).transpose(1, 0, 2)

    def attend(triple):
        q_head, k_head, v_head = triple
        scores = jnp.dot(q_head, k_head.T, preferred_element_type=jnp.float32) * (1.0 / math.sqrt(head_dim))
        peak = lax.optimization_barrier(jnp.max(scores, axis=1, keepdims=True))
        expo = jnp.exp(scores - peak)
        total = lax.optimization_barrier(jnp.sum(expo, axis=1, keepdims=True))
        weights = expo.astype(jnp.bfloat16)
        return (jnp.dot(weights, v_head, preferred_element_type=jnp.float32) / total).astype(jnp.bfloat16)
    context = lax.map(attend, (split_heads(query), split_heads(keys), split_heads(vals)))
    context = context.transpose(1, 0, 2).reshape(TOKENS, D)
    mixed = (wide + jnp.dot(context, w_out, preferred_element_type=jnp.float32)).astype(jnp.bfloat16)
    back = jnp.dot(mixed, w_back, preferred_element_type=jnp.float32)
    out_fields = (fields.astype(jnp.float32) + var_gate.astype(jnp.float32)[:, None, :] * back[None]).astype(jnp.bfloat16)
    return (mixed, out_fields)
```

```python
import functools
import math

import jax
import jax.numpy as jnp
from jax import lax
from jax.experimental import pallas as pl
from jax.experimental.pallas import tpu as pltpu
from jax.sharding import PartitionSpec as P

D = 4096
H = 32
HA = 16
E = 1024
NV = 8
NS = 16
LV = 6
T = 256
W = 512
HD = 128
F32 = jnp.float32
BF = jnp.bfloat16
MESH = pl.DeviceIdType.MESH

VAR_OFF = [(1, 2), (1, 1), (1, 3), (0, 2), (1, 0), (0, 1), (0, 3)]
Z_OFF = [(0, 2), (0, 1), (0, 3)]
Z_NEXT = [(0, 1), (0, 3)]
D_OFF = [(1, 2)] + Z_OFF
SEQ_OFF = [(1, 2), (1, 1), (1, 3), (0, 2), (1, 0), (0, 1), (0, 3)]

A, AF, ST, WX, OX = range(5)
PIECES = 4
WZ = 5
WS = WZ + PIECES
B, C, DG, K, KF, V, VF, Q, CX, XC, F, G, GG = range(WS + PIECES, WS + PIECES + 26, 2)
ROWS = WS + PIECES + 26
TH = T // 2


def rem(a, n):
    return lax.rem(a, jnp.int32(n))


def body(
    fields_h, bias_r, sw_r, av_h, ao_h, gain_r, wq_h, wk_h, wv_h, wo_h, wb_h,
    gate_r,
    mixed_r, back_r, gate_out,
    emb, av, ao, aox, wq, wk, wv, wo, wox, wb,
    e2, prob, stat, cat, bsend, brecv, agg, hid, macc, gsc, gws, off, st1, st2,
    ks, vs, qs, kb, vb, qb, sc, am, al, aa, cs, cb, cbx, fsend, frecv, fown, gsend, grecv, gb,
    ld, ssem, rsem,
):
    me_v = lax.axis_index("var")
    me_s = lax.axis_index("seq")
    xh, z = me_v // 4, rem(me_v, 4)
    xl, y, c = me_s // 8, rem(me_s // 2, 4), rem(me_s, 2)

    def var_of(o, sign=1):
        return rem(xh + o[0], 2) * 4 + rem(z + 4 + sign * o[1], 4)

    def seq_of(o, sign=1):
        return rem(xl + o[0], 2) * 8 + rem(y + 4 + sign * o[1], 4) * 2 + c

    sib = (me_v, xl * 8 + y * 2 + (1 - c))
    near = ((1 - xh) * 4 + z, (1 - xl) * 8 + y * 2 + c)
    part = ((1 - xh) * 4 + z, me_s)

    loads = {}

    def load(name, i, src, dst):
        cp = pltpu.make_async_copy(src, dst, ld.at[i])
        cp.start()
        loads[name] = cp

    av_own = av.at[pl.ds(pl.multiple_of(me_s * 64, 64), 64), :]
    load("av", 0, av_h, av_own)
    load("ao", 2, ao_h, ao)
    load("fields", 1, fields_h, emb)

    bar = pltpu.get_barrier_semaphore()
    for o in VAR_OFF:
        pl.semaphore_signal(bar, inc=1, device_id=(var_of(o), me_s), device_id_type=MESH)
    for o in SEQ_OFF:
        pl.semaphore_signal(bar, inc=1, device_id=(me_v, seq_of(o)), device_id_type=MESH)
    pl.semaphore_signal(bar, inc=1, device_id=sib, device_id_type=MESH)
    pl.semaphore_signal(bar, inc=1, device_id=near, device_id_type=MESH)
    for i in range(1, 4):
        pl.semaphore_signal(
            bar, inc=1, device_id=(part[0], seq_of((0, i))), device_id_type=MESH
        )
    pl.semaphore_wait(bar, 19)

    def remote(src, dst, ph, j, dev):
        return pltpu.make_async_remote_copy(
            src_ref=src, dst_ref=dst, send_sem=ssem.at[ph, j], recv_sem=rsem.at[ph, j],
            device_id=dev, device_id_type=MESH,
        )

    def seq_send(ph, src_of, dst):
        cps = []
        for j, o in enumerate(SEQ_OFF):
            cp = remote(src_of(o), dst(me_s), ph, j, (me_v, seq_of(o)))
            cp.start()
            cps.append(cp)
        return cps

    def seq_forward(ph, cps, dst):
        fw = []
        cp = remote(dst(me_s), dst(me_s), ph, 7, sib)
        cp.start()
        fw.append(cp)
        for j in reversed(range(7)):
            cps[j].wait_recv()
            s = seq_of(SEQ_OFF[j], -1)
            cp = remote(dst(s), dst(s), ph, j, sib)
            cp.start()
            fw.append(cp)
        return fw

    pending = []

    def var_scatter(ph, send, recv):
        cps = []
        for j, o in enumerate(VAR_OFF):
            pv = var_of(o)
            cp = remote(send.at[pv], recv.at[j], ph, j, (pv, me_s))
            cp.start()
            cps.append(cp)
        pending.extend(cps)
        return cps

    def var_gather(ph, buf, offs=VAR_OFF):
        cps = []
        for j, o in enumerate(offs):
            cp = remote(buf.at[me_v], buf.at[me_v], ph, j, (var_of(o), me_s))
            cp.start()
            cps.append(cp)
        pending.extend(cps)
        return cps

    gate_out[...] = gate_r[...].astype(F32)
    for p in range(NV):
        gsc[p] = jnp.broadcast_to(gain_r[p * W : (p + 1) * W].reshape(1, W), (8, W))

    loads["av"].wait()
    av_slot = lambda s: av.at[pl.ds(pl.multiple_of(s * 64, 64), 64), :]
    a_cps = seq_send(A, lambda o: av_slot(me_s), av_slot)
    pending.extend(a_cps)
    load("wk", 3, wk_h, wk)
    load("wv", 4, wv_h, wv)
    load("wq", 5, wq_h, wq)
    load("wo", 6, wo_h, wo)
    load("wb", 7, wb_h, wb)

    PR = E // 2 // PIECES

    def piece(i, core):
        return pl.ds(pl.multiple_of(core * (E // 2) + i * PR, PR), PR)

    loads["ao"].wait()
    wx = []
    for i in range(PIECES):
        cp = remote(ao.at[piece(i, c), :], aox.at[z, piece(i, c), :], WX, i, near)
        cp.start()
        wx.append(cp)
    pending.extend(wx)

    krow = lax.broadcasted_iota(jnp.int32, (128, E), 0)
    kcol = lax.broadcasted_iota(jnp.int32, (128, E), 1)
    e2[...] = jnp.where((rem(krow, 16) == kcol // 64) & (krow < 32), 1.0, 0.0).astype(BF)
    loads["fields"].wait()
    sw = sw_r[...]
    nt = (((1,), (1,)), ((), ()))
    for v in range(LV):
        b = bias_r[v : v + 1, :].astype(F32)

        def embed(r, _, v=v, b=b):
            rows = pl.ds(pl.multiple_of(r * 32, 32), 32)
            emb[v, rows, :] = (emb[v, rows, :].astype(F32) + b).astype(BF)
            return 0

        lax.fori_loop(0, T // 32, embed, 0)
        prob[v] = lax.dot_general(emb[v], sw, nt, preferred_element_type=F32)
    peak = prob[0]
    for v in range(1, LV):
        peak = jnp.maximum(peak, prob[v])
    total = jnp.zeros_like(peak)
    for v in range(LV):
        p = jnp.exp(prob[v] - peak)
        prob[v] = p
        total = total + p
    stat[me_v] = jnp.concatenate(
        [peak, total, jnp.zeros((T, 96), F32)], axis=1
    ).T[:32, :]
    s_cps = var_gather(ST, stat)
    wz = []
    ws = []

    def piece_on(i):
        wx[i].wait_recv()
        rows = piece(i, c)
        for j, o in enumerate(Z_NEXT):
            cp = remote(aox.at[z, rows, :], aox.at[z, rows, :], WZ + i, j, (var_of(o), me_s))
            cp.start()
            wz.append(cp)
            pending.append(cp)
        cp = remote(aox.at[z, rows, :], aox.at[z, rows, :], WS + i, 2, sib)
        cp.start()
        ws.append(cp)
        pending.append(cp)

    for i in range(PIECES):
        piece_on(i)
    a_fw = seq_forward(AF, a_cps, av_slot)
    pending.extend(a_fw)
    for cp in s_cps:
        cp.wait_recv()
    top = stat[0, :16, :]
    for i in range(1, NV):
        top = jnp.maximum(top, stat[i, :16, :])
    tot = jnp.zeros_like(top)
    for i in range(NV):
        tot = tot + stat[i, 16:, :] * jnp.exp(stat[i, :16, :] - top)
    scale = jnp.exp(stat[me_v, :16, :] - top) / tot
    fac = jnp.concatenate([scale, jnp.zeros((112, T), F32)], axis=0).T[:, :16]
    for v in range(LV):
        w = prob[v] * fac
        hi = w.astype(BF).astype(F32)
        cat[v] = jnp.concatenate([hi, w - hi, jnp.zeros((T, 96), F32)], axis=1).astype(BF)
    for cp in a_fw:
        cp.wait_recv()

    def values(hf):
        half = slice(hf * TH, (hf + 1) * TH)
        ev = emb[:, half, :].reshape(LV * TH, E)
        ct = cat[:, half, :].reshape(LV * TH, 128)

        def tile(n, _):
            cols = pl.ds(pl.multiple_of(n * 256, 256), 256)
            wide = jnp.dot(ct, e2[:, cols], preferred_element_type=F32)
            vals = jnp.dot(ev, av[:, cols], preferred_element_type=F32)
            s = jnp.sum((wide * vals).reshape(LV, TH, 256), axis=0).astype(BF)
            bsend[hf, 2 * n] = s[:, :128]
            bsend[hf, 2 * n + 1] = s[:, 128:]
            return 0

        lax.fori_loop(0, 4, tile, 0)

    b_cps = []
    for hf in range(2):
        values(hf)
        b_cps.append(var_scatter(B + hf, bsend.at[hf], brecv.at[hf]))

    loads["wo"].wait()
    mine_rows = pl.ds(pl.multiple_of(c * (W // 2), W // 2), W // 2)
    far_cols = pl.ds(pl.multiple_of((1 - xh) * (D // 2), D // 2), D // 2)
    ox = remote(wo.at[mine_rows, far_cols], wox.at[mine_rows, :], OX, 0, near)
    ox.start()
    pending.append(ox)

    for i in range(PIECES):
        rows = piece(i, c)
        for j, o in enumerate(Z_NEXT):
            wz[2 * i + j].wait_recv()
            zz = rem(z + 4 - o[1], 4)
            cp = remote(aox.at[zz, rows, :], aox.at[zz, rows, :], WS + i, j, sib)
            cp.start()
            ws.append(cp)
            pending.append(cp)

    for name in ("wk", "wv", "wq"):
        loads[name].wait()

    def gain_sums(p, _):
        g = gsc[p]
        hi = g.astype(BF).astype(F32)
        rows = pl.ds(pl.multiple_of(p * W, W), W)
        top = lax.broadcasted_iota(jnp.int32, (16, W), 0) < 8
        g2 = jnp.where(top, jnp.concatenate([hi, hi], axis=0), jnp.concatenate([g - hi, g - hi], axis=0))
        g2 = g2.astype(BF)
        for i, w in enumerate((wk, wv, wq)):
            o = jnp.dot(g2, w[rows, :], preferred_element_type=F32)
            gws[i] = gws[i] + o[0:1, :] + o[8:9, :]
        return 0

    gws[...] = jnp.zeros_like(gws)
    lax.fori_loop(0, NV, gain_sums, 0)

    c_cps = []
    for hf in range(2):
        tot = bsend[hf, me_v].astype(F32)
        for j in reversed(range(7)):
            b_cps[hf][j].wait_recv()
            tot = tot + brecv[hf, j].astype(F32)
        agg[hf, me_v] = tot.astype(BF)
        c_cps.append(var_gather(C + hf, agg.at[hf]))

    d_cps = []
    fulls = []
    for hf in range(2):
        for cp in c_cps[hf]:
            cp.wait_recv()
        full = jnp.concatenate([agg[hf, p] for p in range(NV)], axis=1)
        hid[hf, me_v] = jnp.dot(full, ao[...], preferred_element_type=F32).astype(BF)
        d_cps.append(var_gather(DG + hf, hid.at[hf], D_OFF))
    for cp in ws:
        cp.wait_recv()

    def other_side(i, _):
        zz = rem(z + 3 + i, 4)
        for hf in range(2):
            full = jnp.concatenate([agg[hf, p] for p in range(NV)], axis=1)
            hid[hf, (1 - xh) * 4 + zz] = jnp.dot(
                full, aox[zz], preferred_element_type=F32
            ).astype(BF)
        return 0

    lax.fori_loop(0, 3, other_side, 0)

    def shift(hf):
        t = jnp.zeros((TH, W), F32)
        for i in range(4):
            vv = me_v if i == 3 else (1 - xh) * 4 + rem(z + 3 + i, 4)
            t = t + hid[hf, vv].astype(F32)
        off[hf] = jnp.sum(t, axis=1, keepdims=True) * (1.0 / (4 * W))

    def take(hf, vv, first=False):
        d = hid[hf, vv].astype(F32) - off[hf]
        x = (d * gsc[vv, 0:1, :]).astype(BF)
        rows = pl.ds(pl.multiple_of(vv * W, W), W)
        for i, w in enumerate((wk, wv, wq)):
            o = jnp.dot(x, w[rows, :], preferred_element_type=F32)
            macc[hf, i] = o if first else macc[hf, i] + o
        s1 = d[:, 0:128]
        s2 = s1 * s1
        for n in range(1, 4):
            e = d[:, n * 128 : (n + 1) * 128]
            s1 = s1 + e
            s2 = s2 + e * e
        if not first:
            s1 = s1 + st1[hf]
            s2 = s2 + st2[hf]
        st1[hf] = s1
        st2[hf] = s2

    def statistics(hf):
        mean = jnp.sum(st1[hf], axis=1, keepdims=True) * (1.0 / D)
        sq = jnp.sum(st2[hf], axis=1, keepdims=True) * (1.0 / D)
        return mean, lax.rsqrt(jnp.maximum(sq - mean * mean, 0.0) + 1e-05)

    def project(i, out, hf, mean, inv):
        m = (macc[hf, i] - mean * gws[i]) * inv
        for h in range(4):
            out[hf, h] = m[:, h * HD : (h + 1) * HD].astype(BF)

    def slot(buf, hf):
        return lambda s: buf.at[hf, pl.ds(pl.multiple_of(s * TH, TH), TH), :]

    mine = pl.ds(pl.multiple_of(me_s * TH, TH), TH)

    def send_kv(ph, out, buf, hf):
        cps = seq_send(ph + hf, lambda o: out.at[hf, rem(y + o[1], 4)], slot(buf, hf))
        pending.extend(cps)
        buf[hf, mine, :] = out[hf, y]
        return cps

    def send_q(hf):
        cps = []
        for i in range(1, 4):
            h = rem(y + i, 4)
            cp = remote(
                qs.at[hf, h], qb.at[hf, pl.ds((4 - i) * TH, TH), :], Q + hf, i,
                (me_v, xl * 8 + h * 2 + c),
            )
            cp.start()
            cps.append(cp)
        pending.extend(cps)
        qb[hf, 0:TH, :] = qs[hf, y]
        return cps

    coef = math.log2(math.e) / math.sqrt(HD)
    KC = 512
    NK = NS * TH
    QT = 2 * TH

    def attend(hf, kh):
        def tile(i, _):
            base = 2 * (1 - i)
            rows = pl.ds(pl.multiple_of(base * TH, QT), QT)
            q = qb[hf, rows, :]
            top = None
            for k in range(NK // KC):
                s = lax.dot_general(
                    q, kb[kh, k * KC : (k + 1) * KC, :], nt, preferred_element_type=F32
                )
                sc[:, k * KC : (k + 1) * KC] = s
                top = s if top is None else jnp.maximum(top, s)
            m = jnp.max(top, axis=1, keepdims=True)
            if kh == 1:
                m0 = am[hf, rows, :]
                m = jnp.maximum(m, m0)
                old = jnp.exp2((m0 - m) * coef)
            tot = None
            out = None
            for k in range(NK // KC):
                p = jnp.exp2((sc[:, k * KC : (k + 1) * KC] - m) * coef)
                o = jnp.dot(
                    p.astype(BF), vb[kh, k * KC : (k + 1) * KC, :], preferred_element_type=F32
                )
                tot = p if tot is None else tot + p
                out = o if out is None else out + o
            tot = jnp.sum(tot, axis=1, keepdims=True)
            if kh == 0:
                am[hf, rows, :] = m
                al[hf, rows, :] = tot
                aa[hf, rows, :] = out
                return 0
            tot = tot + al[hf, rows, :] * old
            out = out + aa[hf, rows, :] * old
            res = (out / tot).astype(BF)
            cs[hf, base] = res[:TH]
            cs[hf, base + 1] = res[TH:]
            for k in (base, base + 1):
                src = rem(y + k, 4)
                remote(
                    cs.at[hf, k], cbx.at[hf, y], XC + hf, k, (part[0], xl * 8 + src * 2 + c)
                ).start()

                @pl.when(k != 0)
                def _():
                    remote(
                        cs.at[hf, k], cb.at[hf, y], CX + hf, k, (me_v, xl * 8 + src * 2 + c)
                    ).start()

            return 0

        lax.fori_loop(0, 2, tile, 0)
        if kh == 1:
            cb[hf, y] = cs[hf, 0]
            for k in range(1, 4):
                src = rem(y + k, 4)
                cp = remote(
                    cs.at[hf, k], cb.at[hf, y], CX + hf, k, (me_v, xl * 8 + src * 2 + c)
                )
                cx_cps[hf].append(cp)
            for k in range(4):
                src = rem(y + k, 4)
                cp = remote(
                    cs.at[hf, k], cbx.at[hf, y], XC + hf, k, (part[0], xl * 8 + src * 2 + c)
                )
                cx_cps[hf].append(cp)
            pending.extend(cx_cps[hf])

    cx_cps = [[], []]

    for hf in range(2):
        shift(hf)
        take(hf, me_v, True)

        def local(i, _, hf=hf):
            take(hf, (1 - xh) * 4 + rem(z + 3 + i, 4))
            return 0

        lax.fori_loop(0, 3, local, 0)

    def arrive(hf):
        for j in reversed(range(4)):
            d_cps[hf][j].wait_recv()
            o = D_OFF[j]
            take(hf, var_of(o, -1))

    arrive(0)
    mean, inv = statistics(0)
    project(0, ks, 0, mean, inv)
    k0 = send_kv(K, ks, kb, 0)
    project(1, vs, 0, mean, inv)
    v0 = send_kv(V, vs, vb, 0)
    project(2, qs, 0, mean, inv)
    q0 = send_q(0)

    arrive(1)
    mean, inv = statistics(1)
    project(0, ks, 1, mean, inv)
    k1 = send_kv(K, ks, kb, 1)
    project(1, vs, 1, mean, inv)
    v1 = send_kv(V, vs, vb, 1)
    project(2, qs, 1, mean, inv)
    q1 = send_q(1)
    k0f = seq_forward(KF, k0, slot(kb, 0))
    v0f = seq_forward(VF, v0, slot(vb, 0))
    pending.extend(k0f + v0f)
    ox.wait_recv()
    ox_sib = remote(
        wox.at[mine_rows, :], wox.at[mine_rows, :], OX, 1, sib
    )
    ox_sib.start()
    pending.append(ox_sib)

    for cp in k0f + v0f + q0:
        cp.wait_recv()
    attend(0, 0)
    k1f = seq_forward(KF + 1, k1, slot(kb, 1))
    v1f = seq_forward(VF + 1, v1, slot(vb, 1))
    pending.extend(k1f + v1f)
    for cp in q1:
        cp.wait_recv()
    attend(1, 0)
    for cp in k1f + v1f:
        cp.wait_recv()
    attend(0, 1)
    attend(1, 1)

    ox_sib.wait_recv()
    f_cps = [[], []]
    for hf in range(2):
        for cp in cx_cps[hf]:
            cp.wait_recv()
        ctx = jnp.concatenate([cb[hf, h] for h in range(4)], axis=1)
        ctx2 = jnp.concatenate([cbx[hf, h] for h in range(4)], axis=1)

        def out_block(zz):
            own = pl.ds(pl.multiple_of(xh * (D // 2) + zz * W, W), W)
            oth = pl.ds(pl.multiple_of(zz * W, W), W)
            return jnp.dot(ctx, wo[:, own], preferred_element_type=F32) + jnp.dot(
                ctx2, wox[:, oth], preferred_element_type=F32
            )

        for j, o in enumerate(Z_OFF):
            fsend[hf, j] = out_block(rem(z + o[1], 4)).astype(BF)
            cp = remote(fsend.at[hf, j], frecv.at[hf, j], F + hf, j, (var_of(o), me_s))
            cp.start()
            f_cps[hf].append(cp)
        pending.extend(f_cps[hf])
        fown[hf] = out_block(z) + hid[hf, me_v].astype(F32)

    loads["wb"].wait()
    g_cps = []
    gg_cps = []

    def mix_and_back(hf):
        for cp in f_cps[hf]:
            cp.wait_recv()

        def mix(r, _):
            rows = pl.ds(pl.multiple_of(r * 32, 32), 32)
            s = fown[hf, rows, :]
            for j in range(3):
                s = s + frecv[hf, j, rows, :].astype(F32)
            mixed_r[pl.ds(pl.multiple_of(hf * TH + r * 32, 32), 32), :] = s.astype(BF)
            return 0

        lax.fori_loop(0, TH // 32, mix, 0)
        mx = mixed_r[hf * TH : (hf + 1) * TH, :]
        for p in range(0, NV, 2):
            g = jnp.dot(mx, wb[:, p * 128 : (p + 2) * 128], preferred_element_type=F32)
            gsend[hf, p] = g[:, :128].astype(BF)
            gsend[hf, p + 1] = g[:, 128:].astype(BF)
        g_cps.append(var_scatter(G + hf, gsend.at[hf], grecv.at[hf]))

    def back_sum(hf):
        tot = gsend[hf, me_v].astype(F32)
        for j in reversed(range(7)):
            g_cps[hf][j].wait_recv()
            tot = tot + grecv[hf, j].astype(F32)
        gb[hf, me_v] = tot.astype(BF)
        gg_cps.append(var_gather(GG + hf, gb.at[hf]))

    def back_rows(hf):
        for cp in gg_cps[hf]:
            cp.wait_recv()
        for p in range(NV):
            back_r[hf * TH : (hf + 1) * TH, p * 128 : (p + 1) * 128] = gb[hf, p].astype(F32)

    mix_and_back(0)
    mix_and_back(1)
    back_sum(0)
    back_sum(1)
    back_rows(0)
    back_rows(1)

    for cp in pending:
        cp.wait_send()


def per_device(
    fields, var_bias, agg_score, agg_value, agg_out, norm_gain,
    w_query, w_key, w_value, w_out, w_back, var_gate,
):
    any_spec = pl.BlockSpec(memory_space=pl.ANY)
    vm = pl.BlockSpec(memory_space=pltpu.VMEM)
    mixed, back, gate = pl.pallas_call(
        body,
        out_shape=(
            jax.ShapeDtypeStruct((T, W), BF),
            jax.ShapeDtypeStruct((T, E), F32),
            jax.ShapeDtypeStruct((LV, E), F32),
        ),
        in_specs=[
            any_spec, vm, vm, any_spec, any_spec, vm,
            any_spec, any_spec, any_spec, any_spec, any_spec, vm,
        ],
        out_specs=(vm, vm, vm),
        scratch_shapes=[
            pltpu.VMEM((LV, T, E), BF),
            pltpu.VMEM((E, E), BF),
            pltpu.VMEM((E, W), BF),
            pltpu.VMEM((4, E, W), BF),
            pltpu.VMEM((D, W), BF),
            pltpu.VMEM((D, W), BF),
            pltpu.VMEM((D, W), BF),
            pltpu.VMEM((W, D), BF),
            pltpu.VMEM((W, D // 2), BF),
            pltpu.VMEM((W, E), BF),
            pltpu.VMEM((128, E), BF),
            pltpu.VMEM((LV, T, HA), F32),
            pltpu.VMEM((NV, 32, T), F32),
            pltpu.VMEM((LV, T, 128), BF),
            pltpu.VMEM((2, NV, TH, 128), BF),
            pltpu.VMEM((2, 7, TH, 128), BF),
            pltpu.VMEM((2, NV, TH, 128), BF),
            pltpu.VMEM((2, NV, TH, W), BF),
            pltpu.VMEM((2, 3, TH, W), F32),
            pltpu.VMEM((NV, 8, W), F32),
            pltpu.VMEM((3, 1, W), F32),
            pltpu.VMEM((2, TH, 1), F32),
            pltpu.VMEM((2, TH, 128), F32),
            pltpu.VMEM((2, TH, 128), F32),
            pltpu.VMEM((2, 4, TH, HD), BF),
            pltpu.VMEM((2, 4, TH, HD), BF),
            pltpu.VMEM((2, 4, TH, HD), BF),
            pltpu.VMEM((2, NS * TH, HD), BF),
            pltpu.VMEM((2, NS * TH, HD), BF),
            pltpu.VMEM((2, 4 * TH, HD), BF),
            pltpu.VMEM((2 * TH, NS * TH), F32),
            pltpu.VMEM((2, 4 * TH, 1), F32),
            pltpu.VMEM((2, 4 * TH, 1), F32),
            pltpu.VMEM((2, 4 * TH, HD), F32),
            pltpu.VMEM((2, 4, TH, HD), BF),
            pltpu.VMEM((2, 4, TH, HD), BF),
            pltpu.VMEM((2, 4, TH, HD), BF),
            pltpu.VMEM((2, 3, TH, W), BF),
            pltpu.VMEM((2, 3, TH, W), BF),
            pltpu.VMEM((2, TH, W), F32),
            pltpu.VMEM((2, NV, TH, 128), BF),
            pltpu.VMEM((2, 7, TH, 128), BF),
            pltpu.VMEM((2, NV, TH, 128), BF),
            pltpu.SemaphoreType.DMA((8,)),
            pltpu.SemaphoreType.DMA((ROWS, 8)),
            pltpu.SemaphoreType.DMA((ROWS, 8)),
        ],
        compiler_params=pltpu.CompilerParams(
            collective_id=0, has_side_effects=True, vmem_limit_bytes=60 * 2**20
        ),
    )(
        fields, var_bias, agg_score.T, agg_value, agg_out, norm_gain,
        w_query, w_key, w_value, w_out, w_back, var_gate,
    )
    out_fields = (fields.astype(F32) + gate[:, None, :] * back[None]).astype(BF)
    return (mixed, out_fields)


def solution(mesh):
    in_specs = (
        P("var", "seq", None),
        P("var", None),
        P(),
        P("seq", None),
        P(None, "var"),
        P(),
        P(None, "var"),
        P(None, "var"),
        P(None, "var"),
        P("var", None),
        P("var", None),
        P("var", None),
    )
    out_specs = (P("seq", "var"), P("var", "seq", None))
    return jax.shard_map(
        per_device, mesh=mesh, in_specs=in_specs, out_specs=out_specs, check_vma=False
    )
```
